32 devices in a mesh: snap: 2 (over y), row: 4 (over z), col: 4 (over x, core).
Axes of the slice: x: 2, y: 2, z: 4, core: 2. Of those that a mesh axis runs over, the one named last changes fastest.
Arguments:
- orbitals: float32 [12288, 768], P(('snap', 'row', 'col')), parts along dimension 0, may hold values from -6 to 6
- screened: float32 [6, 6144, 6144], P('snap', 'row', 'col'), parts along dimension 0, may hold values from -0.0029296875 to 0.0029296875
- green_weight: float32 [6, 768], P('snap'), parts along dimension 0, may hold values from 0.05 to 1
- time_weight: float32 [3], replicated, may hold values from 0.3 to 1
Outputs:
- updated: float32 [12288, 768], P(('snap', 'row', 'col')), parts along dimension 0
The draws below stay inside these ranges and needn't reach their ends.
There are 2 independent parts, one for each index of `snap`. The reference program is written for one: setup_inputs(seed, part) draws one part's arguments, and reference() takes and returns one part's arrays. A program takes and returns all parts, laid end to end along the dimension named above; an argument that names none is the same for every part. Nothing has to cross between parts.
All inputs are finite; a program needn't handle non-finite values.
Results may differ from the reference program's by a relative error of at most 0.00013.
Values sent between devices are 32-bit elements; how exact they have to be, the bound alone decides.
No kernel may reach another device: no remote copies, remote signals or barrier semaphores. Data moves between devices by JAX's collectives and lax.ppermute only.
A program may use at most 128 MiB of HBM per device.

```python
import math
import jax
import jax.numpy as jnp
from jax import lax

NP = 6144
NORB = 768
TIMES = 3
PASSES = 2


def level_of(stream_key, shape, split, smallest, high):
    gain = 1.0
    for axis_at, parts in split:
        steps = jax.random.uniform(jax.random.fold_in(jax.random.fold_in(stream_key, 6), axis_at), (parts,), jnp.float32, smallest / len(split), high / len(split))
        gain = gain * jnp.repeat(jnp.exp(steps), shape[axis_at] // parts).reshape((-1,) + (1,) * (len(shape) - 1 - axis_at))
    return gain


def centred(key, dims, scale, bound, cuts=(), dtype=jnp.bfloat16):
    array = jax.random.normal(key, dims, jnp.float32) * scale
    if len(cuts) > 0:
        array = level_of(key, dims, cuts, -0.22, 0.18) * array
    return jnp.clip(array, min=-bound, max=bound).astype(dtype)


def setup_inputs(seed: int = 0, part: int = 0) -> dict:
    streams_of = jax.random.split(jax.random.key(seed), 5)
    part_splits = jax.random.split(jax.random.fold_in(streams_of[4], part), 5)
    orbitals = centred(part_splits[0], (NP, NORB), 1.0, 6.0, ((0, 16),), jnp.float32)
    screened = centred(part_splits[1], (TIMES, NP, NP), (NP * NORB) ** -0.5, 0.0029296875, ((1, 4), (2, 4)), jnp.float32)
    green_weight = jnp.clip(jnp.exp(jax.random.uniform(part_splits[2], (TIMES, NORB), jnp.float32, math.log(0.05), math.log(1.0))), 0.05, 1.0)
    time_weight = jnp.clip(jax.random.uniform(streams_of[3], (TIMES,), jnp.float32, 0.3, 1.0), 0.3, 1.0)
    return dict(orbitals=orbitals, screened=screened, green_weight=green_weight, time_weight=time_weight)


def reference(orbitals, screened, green_weight, time_weight):
    phi = orbitals
    for step in range(PASSES):
        correction = jnp.zeros(phi.shape, jnp.float32)
        for t in range(TIMES):
            green = lax.dot_general(phi * green_weight[t], phi, (((1,), (1,)), ((), ())), precision=lax.Precision.HIGHEST, preferred_element_type=jnp.float32)
            applied = jnp.dot(green * screened[t], phi, precision=lax.Precision.HIGHEST, preferred_element_type=jnp.float32)
            correction = correction + time_weight[t] * applied
        phi = phi - correction
    return phi
```

```python
import functools

import jax
import jax.numpy as jnp
from jax import lax
from jax.experimental import pallas as pl
from jax.experimental.pallas import tpu as pltpu
from jax.sharding import PartitionSpec as P

PASSES = 2
VMEM_BYTES = 60 * 2**20


def dot_t(a, b):
    return lax.dot_general(a, b, (((1,), (1,)), ((), ())), preferred_element_type=jnp.float32)


def dot_n(a, b):
    return lax.dot_general(a, b, (((1,), (0,)), ((), ())), preferred_element_type=jnp.float32)


def split(x):
    high = x.astype(jnp.bfloat16)
    return high, (x - high.astype(jnp.float32)).astype(jnp.bfloat16)


def apply_kernel(first, place, rows_ref, cols_ref, weight_ref, screened_ref, *rest):
    if first:
        out_ref, wh_ref, wl_ref, ch_ref, cl_ref = rest
    else:
        in_ref, out_ref, wh_ref, wl_ref, ch_ref, cl_ref = rest
    times = weight_ref.shape[0]

    @pl.when(pl.program_id(0) == 0)
    def _():
        cols = cols_ref[...]
        ch_ref[...], cl_ref[...] = split(cols)
        for t in range(times):
            wh_ref[t], wl_ref[t] = split(cols * weight_ref[t, :][None, :])

    high, low = split(rows_ref[...])
    mixed = None
    for t in range(times):
        green = dot_t(high, wh_ref[t]) + (dot_t(high, wl_ref[t]) + dot_t(low, wh_ref[t]))
        term = green * screened_ref[t]
        mixed = term if mixed is None else mixed + term
    high, low = split(mixed)
    applied = dot_n(high, ch_ref[...]) + (dot_n(high, cl_ref[...]) + dot_n(low, ch_ref[...]))
    out_ref[...] = applied if first else in_ref[...] + applied


def apply_chunk(place, rows, cols, weight, screened, partial_value, tile):
    n_rows, orbitals = rows.shape
    width = cols.shape[0]
    times = weight.shape[0]
    first = partial_value is None
    tile_spec = pl.BlockSpec((tile, orbitals), lambda i, place: (i, 0))
    in_specs = [
        tile_spec,
        pl.BlockSpec((width, orbitals), lambda i, place: (0, 0)),
        pl.BlockSpec((times, orbitals), lambda i, place: (0, 0)),
        pl.BlockSpec((times, tile, width), lambda i, place: (0, place[i], place[n_rows // tile])),
    ]
    args = [rows, cols, weight, screened]
    if not first:
        in_specs.append(tile_spec)
        args.append(partial_value)
    flops = 2 * n_rows * width * orbitals * 3 * (times + 1)
    return pl.pallas_call(
        functools.partial(apply_kernel, first),
        grid_spec=pltpu.PrefetchScalarGridSpec(
            num_scalar_prefetch=1,
            grid=(n_rows // tile,),
            in_specs=in_specs,
            out_specs=tile_spec,
            scratch_shapes=[
                pltpu.VMEM((times, width, orbitals), jnp.bfloat16),
                pltpu.VMEM((times, width, orbitals), jnp.bfloat16),
                pltpu.VMEM((width, orbitals), jnp.bfloat16),
                pltpu.VMEM((width, orbitals), jnp.bfloat16),
            ],
        ),
        out_shape=jax.ShapeDtypeStruct((n_rows, orbitals), jnp.float32),
        input_output_aliases={} if first else {5: 0},
        compiler_params=pltpu.CompilerParams(vmem_limit_bytes=VMEM_BYTES),
        cost_estimate=pl.CostEstimate(
            flops=flops,
            bytes_accessed=4 * (3 * n_rows * orbitals + times * n_rows * width),
            transcendentals=0,
        ),
        name="apply_chunk",
    )(place, *args)


def swap(value, bit, n_col):
    return lax.ppermute(value, "col", [(i, i ^ bit) for i in range(n_col)])


def gather_relative(own, n_col):
    shards = {0: own}
    bit = n_col // 2
    while bit:
        held = dict(shards)
        for p, shard in held.items():
            shards[p ^ bit] = swap(shard, bit, n_col)
        bit //= 2
    return [shards[p] for p in range(n_col)]


def scatter_relative(parts, n_col):
    bit = 1
    held = dict(enumerate(parts))
    while bit < n_col:
        held = {p: held[p] + swap(held[p ^ bit], bit, n_col) for p in held if not p & bit}
        bit *= 2
    return held[0]


def spread(chunk, n_row, n_col):
    factor = n_col // n_row
    root = lax.axis_index("col") // factor
    total = jnp.where(lax.axis_index("row") == root, chunk, jnp.zeros_like(chunk))
    for way in (1, -1):
        moving = chunk
        for hop in range(n_row - 1):
            pairs = []
            for c in range(n_col):
                at = c // factor + way * hop
                to = at + way
                if 0 <= at < n_row and 0 <= to < n_row:
                    pairs.append((at * n_col + c, to * n_col + c))
            moving = lax.ppermute(moving, ("row", "col"), pairs)
            total = total + moving
    return total


def body(orbitals, screened, green_weight, time_weight):
    n_row = lax.axis_size("row")
    n_col = lax.axis_size("col")
    factor = n_col // n_row
    shard = orbitals.shape[0]
    col_index = lax.axis_index("col")
    weight = green_weight * time_weight[:, None]
    own = orbitals
    fine = factor == 1 and shard % 128 == 0
    for step in range(PASSES):
        if fine:
            shards = gather_relative(own, n_col)
            rows = jnp.concatenate(shards, axis=0)
            row_place = [col_index ^ p for p in range(n_col)]
            partial_value = None
            for q in range(n_col):
                cols = spread(shards[q], n_row, n_col)
                place = jnp.stack(row_place + [col_index ^ q]).astype(jnp.int32)
                partial_value = apply_chunk(place, rows, cols, weight, screened, partial_value, shard)
            parts = [partial_value[p * shard : (p + 1) * shard] for p in range(n_col)]
            own = own - scatter_relative(parts, n_col)
        else:
            rows = lax.all_gather(own, "col", axis=0, tiled=True)
            width = screened.shape[2]
            piece = lax.dynamic_slice_in_dim(rows, col_index % factor * width, width, 0)
            cols = spread(piece, n_row, n_col)
            tile = 8 * max(d for d in range(1, 33) if rows.shape[0] % (8 * d) == 0)
            place = jnp.arange(rows.shape[0] // tile + 1, dtype=jnp.int32) % (rows.shape[0] // tile)
            partial_value = apply_chunk(place, rows, cols, weight, screened, None, tile)
            own = own - lax.psum_scatter(partial_value, "col", scatter_dimension=0, tiled=True)
    return own


def solution(mesh):
    in_specs = (P(("snap", "row", "col"), None), P("snap", "row", "col"), P("snap", None), P())
    out_specs = P(("snap", "row", "col"), None)
    return jax.shard_map(body, mesh=mesh, in_specs=in_specs, out_specs=out_specs, check_vma=False)
```

```python
import functools

import jax
import jax.numpy as jnp
from jax import lax
from jax.experimental import pallas as pl
from jax.experimental.pallas import tpu as pltpu
from jax.sharding import PartitionSpec as P

PASSES = 2
LANES = 128
TILE = 384
VMEM_BYTES = 32 * 2**20


def dot_t(a, b):
    return lax.dot_general(a, b, (((1,), (1,)), ((), ())), preferred_element_type=jnp.float32)


def dot_n(a, b):
    return lax.dot_general(a, b, (((1,), (0,)), ((), ())), preferred_element_type=jnp.float32)


def split(x):
    high = x.astype(jnp.bfloat16)
    return high, (x - high.astype(jnp.float32)).astype(jnp.bfloat16)


def apply_kernel(pieces, first, tiles, place, *refs):
    weight_ref, refs = refs[0], refs[1:]
    rows_refs, refs = refs[: len(tiles)], refs[len(tiles) :]
    cols_refs, refs = refs[:pieces], refs[pieces:]
    screened_refs, refs = refs[:pieces], refs[pieces:]
    out_ref, high_ref, low_ref = refs[-3:]
    times = weight_ref.shape[0]
    width = cols_refs[0].shape[0]
    i = pl.program_id(0)

    @pl.when(i == 0)
    def _():
        for p in range(pieces):
            here = pl.ds(p * width, width)
            high_ref[here, :], low_ref[here, :] = split(cols_refs[p][...])

    rows = rows_refs[0][...]
    start = 0
    for ref, count in zip(rows_refs[1:], tiles):
        start += count
        rows = jnp.where(i >= start, ref[...], rows)
    mixed = None
    for t in range(times):
        high, low = split(rows * weight_ref[t, :][None, :])
        green = dot_t(high, high_ref[...]) + (dot_t(high, low_ref[...]) + dot_t(low, high_ref[...]))
        term = green * jnp.concatenate([ref[t] for ref in screened_refs], axis=1)
        mixed = term if mixed is None else mixed + term
    high, low = split(mixed)
    applied = dot_n(high, high_ref[...]) + (dot_n(high, low_ref[...]) + dot_n(low, high_ref[...]))
    out_ref[...] = applied if first else refs[0][...] + applied


def apply_chunk(row_place, col_place, rows, pieces, weight, screened, partial_value, tile, after=()):
    orbitals = rows[0].shape[1]
    n_rows = sum(r.shape[0] for r in rows)
    n = len(pieces)
    width = pieces[0].shape[0]
    times = weight.shape[0]
    tiles = [r.shape[0] // tile for r in rows]
    total = sum(tiles)
    first = partial_value is None
    place = jnp.stack(list(row_place) + list(col_place)).astype(jnp.int32)
    tile_spec = pl.BlockSpec((tile, orbitals), lambda i, place: (i, 0))
    in_specs = [pl.BlockSpec((times, orbitals), lambda i, place: (0, 0))]
    start = 0
    for count in tiles:
        in_specs.append(
            pl.BlockSpec(
                (tile, orbitals),
                lambda i, place, s=start, c=count: (jnp.clip(i - s, 0, c - 1), 0),
            )
        )
        start += count
    in_specs += [pl.BlockSpec((width, orbitals), lambda i, place: (0, 0))] * n
    in_specs += [
        pl.BlockSpec((times, tile, width), lambda i, place, p=p: (0, place[i], place[total + p]))
        for p in range(n)
    ]
    args = [weight, *rows, *pieces] + [screened] * n
    if not first:
        in_specs.append(tile_spec)
        args.append(partial_value)
    aliases = {} if first else {len(args): 0}
    in_specs += [pl.BlockSpec(memory_space=pl.ANY)] * len(after)
    args += after
    return pl.pallas_call(
        functools.partial(apply_kernel, n, first, tiles),
        grid_spec=pltpu.PrefetchScalarGridSpec(
            num_scalar_prefetch=1,
            grid=(total,),
            in_specs=in_specs,
            out_specs=tile_spec,
            scratch_shapes=[pltpu.VMEM((n * width, orbitals), jnp.bfloat16)] * 2,
        ),
        out_shape=jax.ShapeDtypeStruct((n_rows, orbitals), jnp.float32),
        input_output_aliases=aliases,
        compiler_params=pltpu.CompilerParams(vmem_limit_bytes=VMEM_BYTES),
        cost_estimate=pl.CostEstimate(
            flops=2 * n_rows * n * width * orbitals * 3 * (times + 1),
            bytes_accessed=4 * (3 * n_rows * orbitals + times * n_rows * n * width),
            transcendentals=0,
        ),
        name="apply_chunk",
    )(place, *args)


def pick_kernel(n_in, n_out, which, *refs):
    ins, sem = refs[:n_in], refs[-1]
    outs = refs[len(refs) - 1 - n_out : -1]
    if n_in == 1:
        copies = [pltpu.make_async_copy(ins[0].at[which[p]], outs[p], sem.at[p]) for p in range(n_out)]
        for copy in copies:
            copy.start()
        for copy in copies:
            copy.wait()
        return
    for p in range(n_out):
        for j in range(n_in):

            @pl.when(which[p] == j)
            def _():
                pltpu.make_async_copy(ins[j], outs[p], sem.at[p]).start()

    for p in range(n_out):
        pltpu.make_async_copy(ins[0], outs[p], sem.at[p]).wait()


def pick(values, which, handed=(), after=()):
    value = values[0]
    anywhere = pl.BlockSpec(memory_space=pl.ANY)
    shape = jax.ShapeDtypeStruct(value.shape[-2:], value.dtype)
    n_in, n_out, n_on = len(values), len(which), len(handed)
    out = pl.pallas_call(
        functools.partial(pick_kernel, n_in, n_out),
        grid_spec=pltpu.PrefetchScalarGridSpec(
            num_scalar_prefetch=1,
            grid=(),
            in_specs=[anywhere] * (n_in + n_on + len(after)),
            out_specs=[anywhere] * n_on + [pl.BlockSpec(memory_space=pltpu.VMEM)] * n_out,
            scratch_shapes=[pltpu.SemaphoreType.DMA((n_out,))],
        ),
        out_shape=[shape] * (n_on + n_out),
        input_output_aliases={1 + n_in + j: j for j in range(n_on)},
        cost_estimate=pl.CostEstimate(flops=0, bytes_accessed=8 * n_out * shape.size, transcendentals=0),
        name="pick",
    )(jnp.stack(which).astype(jnp.int32), *values, *handed, *after)
    return out[n_on:], out[:n_on]


def swap(value, bit, n_col):
    return lax.ppermute(value, "col", [(i, i ^ bit) for i in range(n_col)])


def gather_relative(own, n_col):
    shards = {0: own}
    bit = n_col // 2
    while bit:
        held = dict(shards)
        for p, shard in held.items():
            shards[p ^ bit] = swap(shard, bit, n_col)
        bit //= 2
    return [shards[p] for p in range(n_col)]


def scatter_relative(parts, n_col):
    bit = 1
    held = dict(enumerate(parts))
    while bit < len(parts):
        held = {p: held[p] + swap(held[p ^ bit], bit, n_col) for p in held if not p & bit}
        bit *= 2
    return held[0]


def line_hop(up, down, n_row):
    pairs = [(i, i + 1) for i in range(n_row - 1)]
    return lax.ppermute(up, "row", pairs), lax.ppermute(down, "row", [(j, i) for i, j in pairs])


def one_pass(starts, screened, weight, n_row, n_col):
    own = jnp.concatenate(starts, axis=0)
    row_index = lax.axis_index("row")
    col_index = lax.axis_index("col")
    shard = own.shape[0]
    chunks = len(starts)
    half = n_col // 2
    shards = gather_relative(own, n_col)
    place = [(col_index ^ p) * (shard // TILE) + j for p in range(n_col) for j in range(shard // TILE)]
    cut = len(place) // 2
    there = [col_index ^ p for p in range(n_col)]
    away = [row_index - c + n_row - 1 for c in there]

    def apply(h, k, partial_value, after=()):
        col_place = [(col_index ^ p) * chunks + k for p in range(n_col)]
        rows = shards[half:] if h else shards[:half]
        row_place = place[cut:] if h else place[:cut]
        return apply_chunk(
            row_place, col_place, rows, pieces[k], weight, screened, partial_value, TILE, after
        )

    def by_hops(k, first_hop):
        ups, downs = [first_hop[0]], [first_hop[1]]
        for _ in range(n_row - 2):
            up, down = line_hop(ups[-1], downs[-1], n_row)
            ups.append(up)
            downs.append(down)
        return downs[::-1] + [held[k]] + ups

    held = list(starts)
    pieces = []
    high = low = None
    hop = line_hop(held[0], held[0], n_row)
    after = ()
    for k in range(chunks):
        handed = ()
        if k < chunks - 2:
            handed = (*line_hop(held[k + 1], held[k + 1], n_row), *held[k + 2 :])
        if k < chunks - 1 or k == 0:
            picked, handed = pick(by_hops(k, hop), away, handed, after)
        else:
            line = lax.all_gather(held[k], "row", axis=0, tiled=False)
            picked, handed = pick([line], there, handed, after)
        if handed:
            hop, held[k + 2 :] = handed[:2], handed[2:]
        pieces.append([picked[0]] + [swap(picked[p], p, n_col) for p in range(1, n_col)])
        high = apply(1, k, high)
        after = (high,) if k == 0 else (low,)
        if k < chunks - 2:
            low = apply(0, k, low)
    far = scatter_relative([high[p * shard : (p + 1) * shard] for p in range(half)], n_col)
    for k in range(max(chunks - 2, 0), chunks):
        low = apply(0, k, low, (far,))
    across = swap(far, half, n_col)
    new = []
    for k in range(chunks):
        here = [slice(p * shard + k * LANES, p * shard + (k + 1) * LANES) for p in range(half)]
        near = scatter_relative([low[at] for at in here], n_col)
        new.append(starts[k] - (near + across[here[0]]))
    return new


def one_pass_plain(own, screened, weight, n_row, n_col):
    factor = n_col // n_row
    width = screened.shape[2]
    row_index = lax.axis_index("row")
    col_index = lax.axis_index("col")
    rows = lax.all_gather(own, "col", axis=0, tiled=True)
    piece = lax.dynamic_slice_in_dim(rows, col_index % factor * width, width, 0)
    piece = jnp.where(row_index == col_index // factor, piece, jnp.zeros_like(piece))
    piece = lax.psum(piece, "row")
    tile = 8 * max(d for d in range(1, 33) if rows.shape[0] % (8 * d) == 0)
    row_place = list(jnp.arange(rows.shape[0] // tile, dtype=jnp.int32))
    partial_value = apply_chunk(
        row_place, [jnp.int32(0)], [rows], [piece], weight, screened, None, tile
    )
    return own - lax.psum_scatter(partial_value, "col", scatter_dimension=0, tiled=True)


def body(orbitals, screened, green_weight, time_weight):
    n_row = lax.axis_size("row")
    n_col = lax.axis_size("col")
    weight = green_weight * time_weight[:, None]
    shard = orbitals.shape[0]
    if n_row == n_col and n_col & (n_col - 1) == 0 and shard % LANES == 0 and shard % TILE == 0:
        chunks = [orbitals[k : k + LANES] for k in range(0, shard, LANES)]
        for _ in range(PASSES):
            chunks = one_pass(chunks, screened, weight, n_row, n_col)
        return jnp.concatenate(chunks, axis=0)
    phi = orbitals
    for _ in range(PASSES):
        phi = one_pass_plain(phi, screened, weight, n_row, n_col)
    return phi


def solution(mesh):
    in_specs = (P(("snap", "row", "col"), None), P("snap", "row", "col"), P("snap", None), P())
    out_specs = P(("snap", "row", "col"), None)
    return jax.shard_map(body, mesh=mesh, in_specs=in_specs, out_specs=out_specs, check_vma=False)
```

```python
import functools

import jax
import jax.numpy as jnp
from jax import lax
from jax.experimental import pallas as pl
from jax.experimental.pallas import tpu as pltpu
from jax.sharding import PartitionSpec as P

PASSES = 2
LANES = 128
VMEM_BYTES = 32 * 2**20


def dot_t(a, b):
    return lax.dot_general(a, b, (((1,), (1,)), ((), ())), preferred_element_type=jnp.float32)


def dot_n(a, b):
    return lax.dot_general(a, b, (((1,), (0,)), ((), ())), preferred_element_type=jnp.float32)


def split(x):
    high = x.astype(jnp.bfloat16)
    return high, (x - high.astype(jnp.float32)).astype(jnp.bfloat16)


def apply_kernel(pieces, first, tiles, place, *refs):
    weight_ref, refs = refs[0], refs[1:]
    rows_refs, refs = refs[: len(tiles)], refs[len(tiles) :]
    cols_refs, refs = refs[:pieces], refs[pieces:]
    screened_refs, refs = refs[:pieces], refs[pieces:]
    out_ref, high_ref, low_ref = refs[-3:]
    times = weight_ref.shape[0]
    width = cols_refs[0].shape[0]
    i = pl.program_id(0)

    @pl.when(i == 0)
    def _():
        for p in range(pieces):
            here = pl.ds(p * width, width)
            high_ref[here, :], low_ref[here, :] = split(cols_refs[p][...])

    rows = rows_refs[0][...]
    start = 0
    for ref, count in zip(rows_refs[1:], tiles):
        start += count
        rows = jnp.where(i >= start, ref[...], rows)
    weighted = [split(rows * weight_ref[t, :][None, :]) for t in range(times)]
    high = jnp.concatenate([h for h, _ in weighted], axis=0)
    low = jnp.concatenate([l for _, l in weighted], axis=0)
    green = dot_t(high, high_ref[...]) + (dot_t(high, low_ref[...]) + dot_t(low, high_ref[...]))
    tile = rows.shape[0]
    mixed = None
    for t in range(times):
        term = green[t * tile : (t + 1) * tile] * jnp.concatenate([ref[t] for ref in screened_refs], axis=1)
        mixed = term if mixed is None else mixed + term
    high, low = split(mixed)
    applied = dot_n(high, high_ref[...]) + (dot_n(high, low_ref[...]) + dot_n(low, high_ref[...]))
    out_ref[...] = applied if first else refs[0][...] + applied


def apply_chunk(row_place, col_place, rows, pieces, weight, screened, partial_value, tile, after=()):
    orbitals = rows[0].shape[1]
    n = len(pieces)
    width = pieces[0].shape[0]
    times = weight.shape[0]
    tiles = [r.shape[0] // tile for r in rows]
    total = sum(tiles)
    n_rows = total * tile
    first = partial_value is None
    place = jnp.stack(list(row_place) + list(col_place)).astype(jnp.int32)
    tile_spec = pl.BlockSpec((tile, orbitals), lambda i, place: (i, 0))
    in_specs = [pl.BlockSpec((times, orbitals), lambda i, place: (0, 0))]
    start = 0
    for count in tiles:
        in_specs.append(
            pl.BlockSpec(
                (tile, orbitals),
                lambda i, place, s=start, c=count: (jnp.clip(i - s, 0, c - 1), 0),
            )
        )
        start += count
    in_specs += [pl.BlockSpec((width, orbitals), lambda i, place: (0, 0))] * n
    in_specs += [
        pl.BlockSpec((times, tile, width), lambda i, place, p=p: (0, place[i], place[total + p]))
        for p in range(n)
    ]
    args = [weight, *rows, *pieces] + [screened] * n
    if not first:
        in_specs.append(tile_spec)
        args.append(partial_value)
    aliases = {} if first else {len(args): 0}
    in_specs += [pl.BlockSpec(memory_space=pl.ANY)] * len(after)
    args += after
    return pl.pallas_call(
        functools.partial(apply_kernel, n, first, tiles),
        grid_spec=pltpu.PrefetchScalarGridSpec(
            num_scalar_prefetch=1,
            grid=(total,),
            in_specs=in_specs,
            out_specs=tile_spec,
            scratch_shapes=[pltpu.VMEM((n * width, orbitals), jnp.bfloat16)] * 2,
        ),
        out_shape=jax.ShapeDtypeStruct((n_rows, orbitals), jnp.float32),
        input_output_aliases=aliases,
        compiler_params=pltpu.CompilerParams(vmem_limit_bytes=VMEM_BYTES),
        cost_estimate=pl.CostEstimate(
            flops=2 * n_rows * n * width * orbitals * 3 * (times + 1),
            bytes_accessed=4 * (3 * n_rows * orbitals + times * n_rows * n * width),
            transcendentals=0,
        ),
        name="apply_chunk",
    )(place, *args)


def pick_kernel(n_in, sets, n_on, which, *refs):
    n_out = which.shape[0]
    outs, sem = refs[len(refs) - 1 - n_out * sets : -1], refs[-1]
    for s in range(sets):
        ins = refs[s * n_in : (s + 1) * n_in]
        for p in range(n_out):
            out, signal = outs[s * n_out + p], sem.at[s * n_out + p]
            if n_in == 1:
                pltpu.make_async_copy(ins[0].at[which[p]], out, signal).start()
                continue
            for j in range(n_in):

                @pl.when(which[p] == j)
                def _():
                    pltpu.make_async_copy(ins[j], out, signal).start()

    for p, out in enumerate(outs):
        source = refs[0].at[0] if n_in == 1 else refs[0]
        pltpu.make_async_copy(source, out, sem.at[p]).wait()


def pick(sets, which, handed=(), after=()):
    n_in, n_out, n_on = len(sets[0]), len(which), len(handed)
    values = [value for values in sets for value in values]
    total = n_out * len(sets)
    anywhere = pl.BlockSpec(memory_space=pl.ANY)
    shape = jax.ShapeDtypeStruct(values[0].shape[-2:], values[0].dtype)
    out = pl.pallas_call(
        functools.partial(pick_kernel, n_in, len(sets), n_on),
        grid_spec=pltpu.PrefetchScalarGridSpec(
            num_scalar_prefetch=1,
            grid=(),
            in_specs=[anywhere] * (len(values) + n_on + len(after)),
            out_specs=[anywhere] * n_on + [pl.BlockSpec(memory_space=pltpu.VMEM)] * total,
            scratch_shapes=[pltpu.SemaphoreType.DMA((total,))],
        ),
        out_shape=[shape] * (n_on + total),
        input_output_aliases={1 + len(values) + j: j for j in range(n_on)},
        cost_estimate=pl.CostEstimate(flops=0, bytes_accessed=8 * total * shape.size, transcendentals=0),
        name="pick",
    )(jnp.stack(which).astype(jnp.int32), *values, *handed, *after)
    picked = out[n_on:]
    return [picked[s * n_out : (s + 1) * n_out] for s in range(len(sets))], out[:n_on]


def swap(value, bit, n_col):
    return lax.ppermute(value, "col", [(i, i ^ bit) for i in range(n_col)])


def gather_relative(own, n_col):
    shards = {0: own}
    bit = n_col // 2
    while bit:
        for p, shard in list(shards.items()):
            shards[p ^ bit] = swap(shard, bit, n_col)
        bit //= 2
    return [shards[p] for p in range(n_col)]


def scatter_relative(parts, n_col):
    bit = 1
    held = dict(enumerate(parts))
    while bit < len(parts):
        held = {p: held[p] + swap(held[p ^ bit], bit, n_col) for p in held if not p & bit}
        bit *= 2
    return held[0]


def line_hops(found, hops, n_row):
    for hop in hops:
        for way in (1, -1):
            pairs = [(i, i + way) for i in range(n_row) if 0 <= i + way < n_row]
            found[way * hop] = lax.ppermute(found[way * (hop - 1)], "row", pairs)
    return found


def one_pass(chunks, screened, weight, n_row, n_col):
    row_index = lax.axis_index("row")
    col_index = lax.axis_index("col")
    n = len(chunks)
    half = n_col // 2
    shard = sum(chunk.shape[0] for chunk in chunks)
    tile = 8 * max(d for d in range(1, 49) if shard % (8 * d) == 0)
    there = [col_index ^ p for p in range(n_col)]
    away = [row_index - c + n_row - 1 for c in there]
    distances = range(1 - n_row, n_row)

    found = [line_hops({0: chunk}, range(1, n_row), n_row) for chunk in chunks[:2]]
    shards = gather_relative(jnp.concatenate(chunks, axis=0), n_col)
    picked, handed = pick([[f[d] for d in distances] for f in found], away, chunks[2:])

    place = [c * (shard // tile) + i for c in there for i in range(shard // tile)]
    cut = len(place) // 2
    pieces = []

    def apply(upper, k, partial_value, after=()):
        col_place = [c * n + k for c in there]
        rows = shards[half:] if upper else shards[:half]
        row_place = place[cut:] if upper else place[:cut]
        return apply_chunk(row_place, col_place, rows, pieces[k], weight, screened, partial_value, tile, after)

    low = high = None
    for k in range(n):
        if k >= 2:
            line = lax.all_gather(handed[k - 2], "row")
            (fetched,), _ = pick([[line]], there, (), (low,) if k == 2 else (high,))
            picked.append(fetched)
        pieces.append([picked[k][0]] + [swap(picked[k][p], p, n_col) for p in range(1, n_col)])
        high = apply(True, k, high)
        if k < max(n - 2, 1):
            low = apply(False, k, low)
    far = scatter_relative([high[p * shard : (p + 1) * shard] for p in range(half)], n_col)
    for k in range(max(n - 2, 1), n):
        low = apply(False, k, low, (far,))
    across = swap(far, half, n_col)
    new = []
    start = 0
    for chunk in chunks:
        here = [slice(p * shard + start, p * shard + start + chunk.shape[0]) for p in range(half)]
        near = scatter_relative([low[at] for at in here], n_col)
        new.append(chunk - (near + across[here[0]]))
        start += chunk.shape[0]
    return new


def one_pass_plain(own, screened, weight, n_row, n_col):
    factor = n_col // n_row
    width = screened.shape[2]
    row_index = lax.axis_index("row")
    col_index = lax.axis_index("col")
    rows = lax.all_gather(own, "col", axis=0, tiled=True)
    piece = lax.dynamic_slice_in_dim(rows, col_index % factor * width, width, 0)
    piece = jnp.where(row_index == col_index // factor, piece, jnp.zeros_like(piece))
    piece = lax.psum(piece, "row")
    tile = 8 * max(d for d in range(1, 33) if rows.shape[0] % (8 * d) == 0)
    row_place = list(jnp.arange(rows.shape[0] // tile, dtype=jnp.int32))
    partial_value = apply_chunk(
        row_place, [jnp.int32(0)], [rows], [piece], weight, screened, None, tile
    )
    return own - lax.psum_scatter(partial_value, "col", scatter_dimension=0, tiled=True)


def body(orbitals, screened, green_weight, time_weight):
    n_row = lax.axis_size("row")
    n_col = lax.axis_size("col")
    weight = green_weight * time_weight[:, None]
    shard = orbitals.shape[0]
    if n_row == n_col and n_col & (n_col - 1) == 0 and shard % LANES == 0:
        chunks = [orbitals[k : k + LANES] for k in range(0, shard, LANES)]
        for _ in range(PASSES):
            chunks = one_pass(chunks, screened, weight, n_row, n_col)
        return jnp.concatenate(chunks, axis=0)
    phi = orbitals
    for _ in range(PASSES):
        phi = one_pass_plain(phi, screened, weight, n_row, n_col)
    return phi


def solution(mesh):
    in_specs = (P(("snap", "row", "col"), None), P("snap", "row", "col"), P("snap", None), P())
    out_specs = P(("snap", "row", "col"), None)
    return jax.shard_map(body, mesh=mesh, in_specs=in_specs, out_specs=out_specs, check_vma=False)
```

```python
import functools

import jax
import jax.numpy as jnp
from jax import lax
from jax.experimental import pallas as pl
from jax.experimental.pallas import tpu as pltpu
from jax.sharding import PartitionSpec as P

PASSES = 2
LANES = 128
VMEM_BYTES = 32 * 2**20


def dot_t(a, b):
    return lax.dot_general(a, b, (((1,), (1,)), ((), ())), preferred_element_type=jnp.float32)


def dot_n(a, b):
    return lax.dot_general(a, b, (((1,), (0,)), ((), ())), preferred_element_type=jnp.float32)


def split(x):
    high = x.astype(jnp.bfloat16)
    return high, (x - high.astype(jnp.float32)).astype(jnp.bfloat16)


def apply_kernel(pieces, first, tiles, place, *refs):
    weight_ref, refs = refs[0], refs[1:]
    rows_refs, refs = refs[: len(tiles)], refs[len(tiles) :]
    cols_refs, refs = refs[:pieces], refs[pieces:]
    screened_refs, refs = refs[:pieces], refs[pieces:]
    out_ref, high_ref, low_ref = refs[-3:]
    times = weight_ref.shape[0]
    width = cols_refs[0].shape[0]
    i = pl.program_id(0)

    @pl.when(i == 0)
    def _():
        for p in range(pieces):
            here = pl.ds(p * width, width)
            high_ref[here, :], low_ref[here, :] = split(cols_refs[p][...])

    rows = rows_refs[0][...]
    start = 0
    for ref, count in zip(rows_refs[1:], tiles):
        start += count
        rows = jnp.where(i >= start, ref[...], rows)
    weighted = [split(rows * weight_ref[t, :][None, :]) for t in range(times)]
    high = jnp.concatenate([h for h, _ in weighted], axis=0)
    low = jnp.concatenate([l for _, l in weighted], axis=0)
    green = dot_t(high, high_ref[...]) + (dot_t(high, low_ref[...]) + dot_t(low, high_ref[...]))
    tile = rows.shape[0]
    mixed = None
    for t in range(times):
        term = green[t * tile : (t + 1) * tile] * jnp.concatenate([ref[t] for ref in screened_refs], axis=1)
        mixed = term if mixed is None else mixed + term
    high, low = split(mixed)
    applied = dot_n(high, high_ref[...]) + (dot_n(high, low_ref[...]) + dot_n(low, high_ref[...]))
    out_ref[...] = applied if first else refs[0][...] + applied


def apply_chunk(place, row_at, col_at, rows, pieces, weight, screened, partial_value, tile, after=()):
    orbitals = rows[0].shape[1]
    n = len(pieces)
    width = pieces[0].shape[0]
    times = weight.shape[0]
    tiles = [r.shape[0] // tile for r in rows]
    total = sum(tiles)
    n_rows = total * tile
    first = partial_value is None
    tile_spec = pl.BlockSpec((tile, orbitals), lambda i, place: (i, 0))
    in_specs = [pl.BlockSpec((times, orbitals), lambda i, place: (0, 0))]
    start = 0
    for count in tiles:
        in_specs.append(
            pl.BlockSpec(
                (tile, orbitals),
                lambda i, place, s=start, c=count: (jnp.clip(i - s, 0, c - 1), 0),
            )
        )
        start += count
    in_specs += [pl.BlockSpec((width, orbitals), lambda i, place: (0, 0))] * n
    in_specs += [
        pl.BlockSpec((times, tile, width), lambda i, place, p=p: (0, place[row_at + i], place[col_at + p]))
        for p in range(n)
    ]
    args = [weight, *rows, *pieces] + [screened] * n
    if not first:
        in_specs.append(tile_spec)
        args.append(partial_value)
    aliases = {} if first else {len(args): 0}
    in_specs += [pl.BlockSpec(memory_space=pl.ANY)] * len(after)
    args += after
    return pl.pallas_call(
        functools.partial(apply_kernel, n, first, tiles),
        grid_spec=pltpu.PrefetchScalarGridSpec(
            num_scalar_prefetch=1,
            grid=(total,),
            in_specs=in_specs,
            out_specs=tile_spec,
            scratch_shapes=[pltpu.VMEM((n * width, orbitals), jnp.bfloat16)] * 2,
        ),
        out_shape=jax.ShapeDtypeStruct((n_rows, orbitals), jnp.float32),
        input_output_aliases=aliases,
        compiler_params=pltpu.CompilerParams(vmem_limit_bytes=VMEM_BYTES),
        cost_estimate=pl.CostEstimate(
            flops=2 * n_rows * n * width * orbitals * 3 * (times + 1),
            bytes_accessed=4 * (3 * n_rows * orbitals + times * n_rows * n * width),
            transcendentals=0,
        ),
        name="apply_chunk",
    )(place, *args)


def pick_kernel(n_in, sets, first, n_out, which, *refs):
    total = n_out * sets
    held, got, put = refs[-3:]
    outs = refs[len(refs) - 3 - total : -3]
    for s in range(sets):
        ins = refs[s * n_in : (s + 1) * n_in]
        for p in range(n_out):
            at = s * n_out + p
            if n_in == 1:
                pltpu.make_async_copy(ins[0].at[which[first + p]], held.at[at], got.at[at]).start()
                continue
            for j in range(n_in):

                @pl.when(which[first + p] == j)
                def _():
                    pltpu.make_async_copy(ins[j], held.at[at], got.at[at]).start()

    for at in range(total):
        source = refs[0].at[0] if n_in == 1 else refs[0]
        pltpu.make_async_copy(source, held.at[at], got.at[at]).wait()
        pltpu.make_async_copy(held.at[at], outs[at], put.at[at]).start()
    for at in range(total):
        pltpu.make_async_copy(held.at[at], outs[at], put.at[at]).wait()


def pick(sets, which, handed=(), after=()):
    which, first, n_out = which
    n_in, n_on = len(sets[0]), len(handed)
    values = [value for values in sets for value in values]
    total = n_out * len(sets)
    anywhere = pl.BlockSpec(memory_space=pl.ANY)
    shape = jax.ShapeDtypeStruct(values[0].shape[-2:], values[0].dtype)
    out = pl.pallas_call(
        functools.partial(pick_kernel, n_in, len(sets), first, n_out),
        grid_spec=pltpu.PrefetchScalarGridSpec(
            num_scalar_prefetch=1,
            grid=(),
            in_specs=[anywhere] * (len(values) + n_on + len(after)),
            out_specs=[anywhere] * (n_on + total),
            scratch_shapes=[pltpu.VMEM((total, *shape.shape), shape.dtype)]
            + [pltpu.SemaphoreType.DMA((total,))] * 2,
        ),
        out_shape=[shape] * (n_on + total),
        input_output_aliases={1 + len(values) + j: j for j in range(n_on)},
        cost_estimate=pl.CostEstimate(flops=0, bytes_accessed=8 * total * shape.size, transcendentals=0),
        name="pick",
    )(which, *values, *handed, *after)
    picked = out[n_on:]
    return [picked[s * n_out : (s + 1) * n_out] for s in range(len(sets))], out[:n_on]


def swap(value, bit, n_col):
    return lax.ppermute(value, "col", [(i, i ^ bit) for i in range(n_col)])


def gather_relative(own, n_col):
    shards = {0: own}
    bit = n_col // 2
    while bit:
        for p, shard in list(shards.items()):
            shards[p ^ bit] = swap(shard, bit, n_col)
        bit //= 2
    return [shards[p] for p in range(n_col)]


def scatter_relative(parts, n_col):
    bit = 1
    held = dict(enumerate(parts))
    while bit < len(parts):
        held = {p: held[p] + swap(held[p ^ bit], bit, n_col) for p in held if not p & bit}
        bit *= 2
    return held[0]


def line_hops(found, hops, n_row):
    for hop in hops:
        for way in (1, -1):
            pairs = [(i, i + way) for i in range(n_row) if 0 <= i + way < n_row]
            found[way * hop] = lax.ppermute(found[way * (hop - 1)], "row", pairs)
    return found


def one_pass(chunks, screened, weight, n_row, n_col):
    row_index = lax.axis_index("row")
    col_index = lax.axis_index("col")
    n = len(chunks)
    half = n_col // 2
    shard = sum(chunk.shape[0] for chunk in chunks)
    tile = 8 * max(d for d in range(1, 49) if shard % (8 * d) == 0)
    there = [col_index ^ p for p in range(n_col)]
    away = [row_index - c + n_row - 1 for c in there]
    distances = range(1 - n_row, n_row)
    place = [c * (shard // tile) + i for c in there for i in range(shard // tile)]
    place += [c * n + k for k in range(n) for c in there]
    place = jnp.stack(place + there + away).astype(jnp.int32)
    there_at = len(there) * (shard // tile + n)
    away_at = there_at + n_col

    found = [line_hops({0: chunk}, range(1, n_row), n_row) for chunk in chunks[:2]]
    shards = gather_relative(jnp.concatenate(chunks, axis=0), n_col)
    picked, handed = pick([[f[d] for d in distances] for f in found], (place, away_at, n_col), chunks[2:])

    tiles = n_col * (shard // tile)
    pieces = []

    def apply(upper, k, partial_value, after=()):
        rows = shards[half:] if upper else shards[:half]
        row_at = tiles // 2 if upper else 0
        col_at = tiles + k * n_col
        return apply_chunk(place, row_at, col_at, rows, pieces[k], weight, screened, partial_value, tile, after)

    low = high = None
    for k in range(n):
        if k >= 2:
            line = lax.all_gather(handed[k - 2], "row")
            (fetched,), _ = pick([[line]], (place, there_at, n_col), (), (low,) if k == 2 else (high,))
            picked.append(fetched)
        pieces.append([picked[k][0]] + [swap(picked[k][p], p, n_col) for p in range(1, n_col)])
        high = apply(True, k, high)
        if k < max(n - 2, 1):
            low = apply(False, k, low)
    far = scatter_relative([high[p * shard : (p + 1) * shard] for p in range(half)], n_col)
    for k in range(max(n - 2, 1), n):
        low = apply(False, k, low, (far,))
    across = swap(far, half, n_col)
    new = []
    start = 0
    for chunk in chunks:
        here = [slice(p * shard + start, p * shard + start + chunk.shape[0]) for p in range(half)]
        near = scatter_relative([low[at] for at in here], n_col)
        new.append(chunk - (near + across[here[0]]))
        start += chunk.shape[0]
    return new


def one_pass_plain(own, screened, weight, n_row, n_col):
    factor = n_col // n_row
    width = screened.shape[2]
    row_index = lax.axis_index("row")
    col_index = lax.axis_index("col")
    rows = lax.all_gather(own, "col", axis=0, tiled=True)
    piece = lax.dynamic_slice_in_dim(rows, col_index % factor * width, width, 0)
    piece = jnp.where(row_index == col_index // factor, piece, jnp.zeros_like(piece))
    piece = lax.psum(piece, "row")
    tile = 8 * max(d for d in range(1, 33) if rows.shape[0] % (8 * d) == 0)
    tiles = rows.shape[0] // tile
    place = jnp.arange(tiles + 1, dtype=jnp.int32) % tiles
    partial_value = apply_chunk(place, 0, tiles, [rows], [piece], weight, screened, None, tile)
    return own - lax.psum_scatter(partial_value, "col", scatter_dimension=0, tiled=True)


def body(orbitals, screened, green_weight, time_weight):
    n_row = lax.axis_size("row")
    n_col = lax.axis_size("col")
    weight = green_weight * time_weight[:, None]
    shard = orbitals.shape[0]
    if n_row == n_col and n_col & (n_col - 1) == 0 and shard % LANES == 0:
        chunks = [orbitals[k : k + LANES] for k in range(0, shard, LANES)]
        for _ in range(PASSES):
            chunks = one_pass(chunks, screened, weight, n_row, n_col)
        return jnp.concatenate(chunks, axis=0)
    phi = orbitals
    for _ in range(PASSES):
        phi = one_pass_plain(phi, screened, weight, n_row, n_col)
    return phi


def solution(mesh):
    in_specs = (P(("snap", "row", "col"), None), P("snap", "row", "col"), P("snap", None), P())
    out_specs = P(("snap", "row", "col"), None)
    return jax.shard_map(body, mesh=mesh, in_specs=in_specs, out_specs=out_specs, check_vma=False)
```

```python
import functools

import jax
import jax.numpy as jnp
from jax import lax
from jax.experimental import pallas as pl
from jax.experimental.pallas import tpu as pltpu
from jax.sharding import PartitionSpec as P

PASSES = 2
LANES = 128
VMEM_BYTES = 32 * 2**20


def dot_t(a, b):
    return lax.dot_general(a, b, (((1,), (1,)), ((), ())), preferred_element_type=jnp.float32)


def dot_n(a, b):
    return lax.dot_general(a, b, (((1,), (0,)), ((), ())), preferred_element_type=jnp.float32)


def split(x):
    high = x.astype(jnp.bfloat16)
    return high, (x - high.astype(jnp.float32)).astype(jnp.bfloat16)


def apply_kernel(pieces, first, tiles, place, *refs):
    weight_ref, refs = refs[0], refs[1:]
    rows_refs, refs = refs[: len(tiles)], refs[len(tiles) :]
    cols_refs, refs = refs[:pieces], refs[pieces:]
    screened_refs, refs = refs[:pieces], refs[pieces:]
    out_ref, high_ref, low_ref = refs[-3:]
    times = weight_ref.shape[0]
    width = cols_refs[0].shape[0]
    i = pl.program_id(0)

    @pl.when(i == 0)
    def _():
        for p in range(pieces):
            here = pl.ds(p * width, width)
            high_ref[here, :], low_ref[here, :] = split(cols_refs[p][...])

    rows = rows_refs[0][...]
    start = 0
    for ref, count in zip(rows_refs[1:], tiles):
        start += count
        rows = jnp.where(i >= start, ref[...], rows)
    weighted = [split(rows * weight_ref[t, :][None, :]) for t in range(times)]
    high = jnp.concatenate([h for h, _ in weighted], axis=0)
    low = jnp.concatenate([l for _, l in weighted], axis=0)
    green = dot_t(high, high_ref[...]) + (dot_t(high, low_ref[...]) + dot_t(low, high_ref[...]))
    tile = rows.shape[0]
    mixed = None
    for t in range(times):
        term = green[t * tile : (t + 1) * tile] * jnp.concatenate([ref[t] for ref in screened_refs], axis=1)
        mixed = term if mixed is None else mixed + term
    high, low = split(mixed)
    applied = dot_n(high, high_ref[...]) + (dot_n(high, low_ref[...]) + dot_n(low, high_ref[...]))
    out_ref[...] = applied if first else refs[0][...] + applied


def apply_chunk(place, row_at, col_at, rows, pieces, weight, screened, partial_value, tile, after=()):
    orbitals = rows[0].shape[1]
    n = len(pieces)
    width = pieces[0].shape[0]
    times = weight.shape[0]
    tiles = [r.shape[0] // tile for r in rows]
    total = sum(tiles)
    n_rows = total * tile
    first = partial_value is None
    tile_spec = pl.BlockSpec((tile, orbitals), lambda i, place: (i, 0))
    in_specs = [pl.BlockSpec((times, orbitals), lambda i, place: (0, 0))]
    start = 0
    for count in tiles:
        in_specs.append(
            pl.BlockSpec(
                (tile, orbitals),
                lambda i, place, s=start, c=count: (jnp.clip(i - s, 0, c - 1), 0),
            )
        )
        start += count
    in_specs += [pl.BlockSpec((width, orbitals), lambda i, place: (0, 0))] * n
    in_specs += [
        pl.BlockSpec((times, tile, width), lambda i, place, p=p: (0, place[row_at + i], place[col_at + p]))
        for p in range(n)
    ]
    args = [weight, *rows, *pieces] + [screened] * n
    if not first:
        in_specs.append(tile_spec)
        args.append(partial_value)
    aliases = {} if first else {len(args): 0}
    in_specs += [pl.BlockSpec(memory_space=pl.ANY)] * len(after)
    args += after
    return pl.pallas_call(
        functools.partial(apply_kernel, n, first, tiles),
        grid_spec=pltpu.PrefetchScalarGridSpec(
            num_scalar_prefetch=1,
            grid=(total,),
            in_specs=in_specs,
            out_specs=tile_spec,
            scratch_shapes=[pltpu.VMEM((n * width, orbitals), jnp.bfloat16)] * 2,
        ),
        out_shape=jax.ShapeDtypeStruct((n_rows, orbitals), jnp.float32),
        input_output_aliases=aliases,
        compiler_params=pltpu.CompilerParams(vmem_limit_bytes=VMEM_BYTES),
        cost_estimate=pl.CostEstimate(
            flops=2 * n_rows * n * width * orbitals * 3 * (times + 1),
            bytes_accessed=4 * (3 * n_rows * orbitals + times * n_rows * n * width),
            transcendentals=0,
        ),
        name="apply_chunk",
    )(place, *args)


def pick_kernel(n_in, sets, first, n_out, which, *refs):
    total = n_out * sets
    held, got, put = refs[-3:]
    outs = refs[len(refs) - 3 - total : -3]
    for s in range(sets):
        ins = refs[s * n_in : (s + 1) * n_in]
        for p in range(n_out):
            at = s * n_out + p
            if n_in == 1:
                pltpu.make_async_copy(ins[0].at[which[first + p]], held.at[at], got.at[at]).start()
                continue
            for j in range(n_in):

                @pl.when(which[first + p] == j)
                def _():
                    pltpu.make_async_copy(ins[j], held.at[at], got.at[at]).start()

    for at in range(total):
        source = refs[0].at[0] if n_in == 1 else refs[0]
        pltpu.make_async_copy(source, held.at[at], got.at[at]).wait()
        pltpu.make_async_copy(held.at[at], outs[at], put.at[at]).start()
    for at in range(total):
        pltpu.make_async_copy(held.at[at], outs[at], put.at[at]).wait()


def pick(sets, which, handed=(), after=()):
    which, first, n_out = which
    n_in, n_on = len(sets[0]), len(handed)
    values = [value for values in sets for value in values]
    total = n_out * len(sets)
    anywhere = pl.BlockSpec(memory_space=pl.ANY)
    shape = jax.ShapeDtypeStruct(values[0].shape[-2:], values[0].dtype)
    out = pl.pallas_call(
        functools.partial(pick_kernel, n_in, len(sets), first, n_out),
        grid_spec=pltpu.PrefetchScalarGridSpec(
            num_scalar_prefetch=1,
            grid=(),
            in_specs=[anywhere] * (len(values) + n_on + len(after)),
            out_specs=[anywhere] * (n_on + total),
            scratch_shapes=[pltpu.VMEM((total, *shape.shape), shape.dtype)]
            + [pltpu.SemaphoreType.DMA((total,))] * 2,
        ),
        out_shape=[shape] * (n_on + total),
        input_output_aliases={1 + len(values) + j: j for j in range(n_on)},
        cost_estimate=pl.CostEstimate(flops=0, bytes_accessed=8 * total * shape.size, transcendentals=0),
        name="pick",
    )(which, *values, *handed, *after)
    picked = out[n_on:]
    return [picked[s * n_out : (s + 1) * n_out] for s in range(len(sets))], out[:n_on]


def swap(value, bit, n_col):
    return lax.ppermute(value, "col", [(i, i ^ bit) for i in range(n_col)])


def gather_relative(own, n_col):
    shards = {0: own}
    bit = n_col // 2
    while bit:
        for p, shard in list(shards.items()):
            shards[p ^ bit] = swap(shard, bit, n_col)
        bit //= 2
    return [shards[p] for p in range(n_col)]


def scatter_relative(parts, n_col):
    bit = 1
    held = dict(enumerate(parts))
    while bit < len(parts):
        held = {p: held[p] + swap(held[p ^ bit], bit, n_col) for p in held if not p & bit}
        bit *= 2
    return held[0]


def join_kernel(n, *refs):
    out_ref = refs[-1]
    start = 0
    for ref in refs[:n]:
        out_ref[start : start + ref.shape[0], :] = ref[...]
        start += ref.shape[0]


def join(values, after):
    rows = sum(value.shape[0] for value in values)
    shape = jax.ShapeDtypeStruct((rows, values[0].shape[1]), values[0].dtype)
    vmem = pl.BlockSpec(memory_space=pltpu.VMEM)
    return pl.pallas_call(
        functools.partial(join_kernel, len(values)),
        in_specs=[vmem] * len(values) + [pl.BlockSpec(memory_space=pl.ANY)] * len(after),
        out_specs=vmem,
        out_shape=shape,
        cost_estimate=pl.CostEstimate(flops=0, bytes_accessed=8 * shape.size, transcendentals=0),
        name="join",
    )(*values, *after)


def line_hops(found, hops, n_row):
    for hop in hops:
        for way in (1, -1):
            pairs = [(i, i + way) for i in range(n_row) if 0 <= i + way < n_row]
            found[way * hop] = lax.ppermute(found[way * (hop - 1)], "row", pairs)
    return found


def one_pass(chunks, screened, weight, n_row, n_col):
    row_index = lax.axis_index("row")
    col_index = lax.axis_index("col")
    n = len(chunks)
    half = n_col // 2
    shard = sum(chunk.shape[0] for chunk in chunks)
    tile = 8 * max(d for d in range(1, 49) if shard % (8 * d) == 0)
    there = [col_index ^ p for p in range(n_col)]
    away = [row_index - c + n_row - 1 for c in there]
    distances = range(1 - n_row, n_row)
    place = [c * (shard // tile) + i for c in there for i in range(shard // tile)]
    place += [c * n + k for k in range(n) for c in there]
    place = jnp.stack(place + there + away).astype(jnp.int32)
    there_at = len(there) * (shard // tile + n)
    away_at = there_at + n_col

    found = [line_hops({0: chunk}, range(1, n_row), n_row) for chunk in chunks[:2]]
    shards = gather_relative(jnp.concatenate(chunks, axis=0), n_col)
    begun = [found[-1][d] for d in (2, -2) if d in found[-1]]
    handed = [join([chunk], begun) for chunk in chunks[2:]]
    picked, _ = pick([[f[d] for d in distances] for f in found], (place, away_at, n_col))

    tiles = n_col * (shard // tile)
    pieces = []

    def apply(upper, k, partial_value, after=()):
        rows = shards[half:] if upper else shards[:half]
        row_at = tiles // 2 if upper else 0
        col_at = tiles + k * n_col
        return apply_chunk(place, row_at, col_at, rows, pieces[k], weight, screened, partial_value, tile, after)

    low = high = None
    for k in range(n):
        pieces.append([picked[k][0]] + [swap(picked[k][p], p, n_col) for p in range(1, n_col)])
        high = apply(True, k, high, picked[k + 1][:1] if 0 < k < n - 1 else ())
        if k + 2 < n:
            line = lax.all_gather(handed[k], "row")
            (fetched,), _ = pick([[line]], (place, there_at, n_col), (), (high,))
            picked.append(fetched)
        if k < max(n - 2, 1):
            low = apply(False, k, low)
    far = scatter_relative([high[p * shard : (p + 1) * shard] for p in range(half)], n_col)
    for k in range(max(n - 2, 1), n):
        low = apply(False, k, low, (far,))
    across = swap(far, half, n_col)
    new = []
    start = 0
    for chunk in chunks:
        here = [slice(p * shard + start, p * shard + start + chunk.shape[0]) for p in range(half)]
        near = scatter_relative([low[at] for at in here], n_col)
        new.append(chunk - (near + across[here[0]]))
        start += chunk.shape[0]
    return new


def one_pass_plain(own, screened, weight, n_row, n_col):
    factor = n_col // n_row
    width = screened.shape[2]
    row_index = lax.axis_index("row")
    col_index = lax.axis_index("col")
    rows = lax.all_gather(own, "col", axis=0, tiled=True)
    piece = lax.dynamic_slice_in_dim(rows, col_index % factor * width, width, 0)
    piece = jnp.where(row_index == col_index // factor, piece, jnp.zeros_like(piece))
    piece = lax.psum(piece, "row")
    tile = 8 * max(d for d in range(1, 33) if rows.shape[0] % (8 * d) == 0)
    tiles = rows.shape[0] // tile
    place = jnp.arange(tiles + 1, dtype=jnp.int32) % tiles
    partial_value = apply_chunk(place, 0, tiles, [rows], [piece], weight, screened, None, tile)
    return own - lax.psum_scatter(partial_value, "col", scatter_dimension=0, tiled=True)


def body(orbitals, screened, green_weight, time_weight):
    n_row = lax.axis_size("row")
    n_col = lax.axis_size("col")
    weight = green_weight * time_weight[:, None]
    shard = orbitals.shape[0]
    if n_row == n_col and n_col & (n_col - 1) == 0 and shard % LANES == 0:
        chunks = [orbitals[k : k + LANES] for k in range(0, shard, LANES)]
        for _ in range(PASSES):
            chunks = one_pass(chunks, screened, weight, n_row, n_col)
        return jnp.concatenate(chunks, axis=0)
    phi = orbitals
    for _ in range(PASSES):
        phi = one_pass_plain(phi, screened, weight, n_row, n_col)
    return phi


def solution(mesh):
    in_specs = (P(("snap", "row", "col"), None), P("snap", "row", "col"), P("snap", None), P())
    out_specs = P(("snap", "row", "col"), None)
    return jax.shard_map(body, mesh=mesh, in_specs=in_specs, out_specs=out_specs, check_vma=False)
```
